32 devices in a mesh: seq: 2 (over x), ctx: 16 (over z, y, core).
Axes of the slice: x: 2, y: 2, z: 4, core: 2. Of those that a mesh axis runs over, the one named last changes fastest.
Arguments:
- tokens: bfloat16 [2, 2048, 2048], P('seq', 'ctx'), may hold values from -80 to 80
- qkv_weight: bfloat16 [2048, 1536], P(None, 'seq'), may hold values from -0.125 to 0.125
- doc_lengths: int32 [2, 12], P('seq'), may hold values from 1 to 256, 2048 in all within a row
- span_order: int32 [2, 32], P('seq'), may hold values from 0 to 31, as said below
Outputs:
- attended: bfloat16 [2, 2048, 1024], P('seq', 'ctx')
The draws below stay inside these ranges and needn't reach their ends.
Inputs may be any that keep to these rules, and one draw needn't show every extreme that they name: `doc_lengths`: each row sums to 2048; its largest entry is exactly 256. `span_order`: in each row, slots 2 i and 2 i + 1 hold spans i and 31 - i, in an order drawn for each pair.
All inputs are finite; a program needn't handle non-finite values.
Results may differ from the reference program's by a relative error of at most 0.012.
The reference program's roundings to bfloat16 on the way count: a program that leaves them out, or rounds other values in their place, can miss the bound.
Values may be sent and summed in bfloat16 or wider, within the bound.
A program may use at most 192 MiB of HBM per device.

```python
import math
import jax
import jax.numpy as jnp
import numpy as np
from jax import lax

D = 2048
QUERY_HEADS = 16
KEY_VALUE_HEADS = 4
HEAD_SIZE = 64
QUERY_PER_KV = 4
QKV = 1536
SPAN = 64
SEQS = 2
LEN = 2048
SPANS = 32
DOC_MOST = 256
DOCS = 12


def draw_tokens(key, part):
    first = jax.random.fold_in(key, 0)
    value_rows = jax.random.normal(first, (SEQS, LEN, D), jnp.float32)
    return jnp.clip(value_rows, -80.0, 80.0).astype(jnp.bfloat16)


def draw_span_order(key, part):
    pairs = SPANS // 2
    flips = jax.random.randint(jax.random.fold_in(key, 7), (SEQS, pairs), 0, 2).astype(jnp.int32)
    early = jnp.broadcast_to(jnp.arange(pairs, dtype=jnp.int32)[None, :], (SEQS, pairs))
    late = (SPANS - 1 - early).astype(jnp.int32)
    first_slot = jnp.where(flips == 1, late, early)
    second_slot = jnp.where(flips == 1, early, late)
    return jnp.stack([first_slot, second_slot], axis=-1).reshape(SEQS, SPANS).astype(jnp.int32)


def steps_of(key, extent, shards, low, largest):
    def one(axis_at, blocks):
        steps = jax.random.uniform(jax.random.fold_in(jax.random.fold_in(key, 6), axis_at), (blocks,), jnp.float32, low / len(shards), largest / len(shards))
        return jnp.repeat(jnp.exp(steps), extent[axis_at] // blocks).reshape((-1,) + (1,) * (len(extent) - axis_at - 1))

    gain = one(*shards[0])
    for cut in shards[1:]:
        gain = gain * one(*cut)
    return gain


def length_profile(number_of, total, limit, skew):
    portions = [(1 << 20) // math.isqrt(grade ** skew) + 1 for grade in range(2, number_of + 1)]
    rest, holding = total - limit - (number_of - 1), [1] * (number_of - 1)
    while rest > 0:
        free = [i for i in range(number_of - 1) if holding[i] < limit]
        pool, budget = sum([portions[i] for i in free]), rest
        for i in free:
            extra = min(limit - holding[i], max(1, budget * portions[i] // pool), rest)
            holding[i] = holding[i] + extra
            rest = rest - extra
    return np.array([limit] + holding)


def uneven_parts(own_key, count, total, most, slope):
    if count == 2:
        one = jax.random.randint(own_key, (), max(1, total - most), min(most, total - 1) + 1)
        return jnp.stack([one, total - one])
    lengths = jnp.asarray(length_profile(count, total, most, slope), jnp.int32)
    pairs = (count - 1) // 2
    donor, receiver = lengths[1:1 + 2 * pairs:2], lengths[2:2 + 2 * pairs:2]
    margin = jnp.minimum(donor - 1, most - receiver)
    passed = jax.random.randint(jax.random.fold_in(own_key, 1), (pairs,), 0, 1 << 20) % (margin + 1)
    lengths = lengths.at[1:1 + 2 * pairs:2].set(donor - passed).at[2:2 + 2 * pairs:2].set(receiver + passed)
    return lengths[jax.random.permutation(jax.random.fold_in(own_key, 2), count)]


def normal_values(rng, shape, deviation, limit, pieces=(), held_as=jnp.bfloat16):
    values = jax.random.normal(rng, shape, jnp.float32) * deviation
    if len(pieces) > 0:
        values = steps_of(rng, shape, pieces, -0.22, 0.18) * values
    return jnp.clip(values, min=-limit, max=limit).astype(held_as)


def setup_inputs(seed: int = 0) -> dict:
    splits = jax.random.split(jax.random.key(seed), 5)
    return {
        "tokens": draw_tokens(jax.random.fold_in(splits[4], 71), 0),
        "qkv_weight": normal_values(splits[1], (D, QKV), D ** -0.5, 0.125, ((1, 2),)),
        "doc_lengths": jax.vmap(lambda own: uneven_parts(own, DOCS, LEN, DOC_MOST, 2))(jax.random.split(splits[2], SEQS)).reshape((SEQS, DOCS)).astype(jnp.int32),
        "span_order": draw_span_order(jax.random.fold_in(splits[4], 71), 0),
    }


def apply_rotary(value_rows, token_positions):
    token_count = value_rows.shape[0]
    heads = value_rows.reshape(token_count, -1, HEAD_SIZE)
    half = HEAD_SIZE // 2
    freq = 500000.0 ** (-jnp.arange(half, dtype=jnp.float32) * 2.0 / HEAD_SIZE)
    angle = token_positions.astype(jnp.float32)[:, None] * freq[None, :]
    cosine = jnp.cos(angle)[:, None, :]
    sine = jnp.sin(angle)[:, None, :]
    first = heads[..., :half]
    second = heads[..., half:]
    turned = jnp.concatenate([first * cosine - second * sine, second * cosine + first * sine], axis=-1)
    return turned.reshape(token_count, -1)


def positions(order_row):
    offsets = jnp.arange(SPAN, dtype=jnp.int32)
    return (order_row[:, None] * SPAN + offsets[None, :]).reshape(-1).astype(jnp.int32)


def documents(lengths_row, token_positions):
    ends = jnp.cumsum(lengths_row).astype(jnp.int32)
    return jnp.sum((ends[None, :] <= token_positions[:, None]).astype(jnp.int32), axis=1)


def one_sequence(rows, lengths_row, order_row, qkv_weight):
    token_positions = positions(order_row)
    docs = documents(lengths_row, token_positions)
    query_key_value = jnp.dot(rows, qkv_weight, preferred_element_type=jnp.float32).astype(jnp.bfloat16)
    query_rows = apply_rotary(query_key_value[:, :QUERY_HEADS * HEAD_SIZE].astype(jnp.float32), token_positions).astype(jnp.bfloat16)
    key_rows = apply_rotary(query_key_value[:, QUERY_HEADS * HEAD_SIZE:(QUERY_HEADS + KEY_VALUE_HEADS) * HEAD_SIZE].astype(jnp.float32), token_positions).astype(jnp.bfloat16)
    value_rows = query_key_value[:, (QUERY_HEADS + KEY_VALUE_HEADS) * HEAD_SIZE:]
    live = (docs[:, None] == docs[None, :]) & (token_positions[None, :] <= token_positions[:, None])

    def one_head(head):
        group = head // QUERY_PER_KV
        query_h = lax.dynamic_slice_in_dim(query_rows, head * HEAD_SIZE, HEAD_SIZE, 1)
        key_h = lax.dynamic_slice_in_dim(key_rows, group * HEAD_SIZE, HEAD_SIZE, 1)
        value_h = lax.dynamic_slice_in_dim(value_rows, group * HEAD_SIZE, HEAD_SIZE, 1)
        scores = jnp.dot(query_h, key_h.T, preferred_element_type=jnp.float32) * 0.125
        scores = jnp.where(live, scores, -1e30)
        top = jnp.max(scores, axis=1, keepdims=True)
        weights = jnp.where(live, jnp.exp(scores - top), 0.0)
        total = jnp.sum(weights, axis=1, keepdims=True)
        summed = jnp.dot(weights.astype(jnp.bfloat16), value_h, preferred_element_type=jnp.float32)
        return summed / total

    outputs = lax.map(one_head, jnp.arange(QUERY_HEADS, dtype=jnp.int32))
    return jnp.transpose(outputs, (1, 0, 2)).reshape(LEN, QUERY_HEADS * HEAD_SIZE).astype(jnp.bfloat16)


def reference(tokens, qkv_weight, doc_lengths, span_order):
    results = []
    for index in range(SEQS):
        results.append(one_sequence(tokens[index], doc_lengths[index], span_order[index], qkv_weight))
    return jnp.stack(results, axis=0)
```

```python
import functools
import math

import jax
import jax.numpy as jnp
import numpy as np
from jax import lax
from jax.experimental import pallas as pl
from jax.experimental.pallas import tpu as pltpu
from jax.sharding import PartitionSpec as P

QUERY_HEADS = 16
KEY_VALUE_HEADS = 4
HEAD_SIZE = 64
QUERY_PER_KV = 4
SPAN = 64
PAIR = 2 * HEAD_SIZE
QCOLS = QUERY_HEADS * HEAD_SIZE
KVCOLS = KEY_VALUE_HEADS * HEAD_SIZE
MESH = pl.DeviceIdType.MESH
SCALE = 0.125 * math.log2(math.e)


def kernel(
    parts, devices, steps, chunks, col_tile,
    tok_ref, w_ref, freq_ref, len_ref, order_ref, out_ref,
    tok_own, w_v, tok_in, back, full, pieces, kv, q_s, bias, cos_s, sin_s,
    local_sem, tok_send, tok_recv, back_send, back_recv, kv_send, kv_recv,
):
    me = lax.axis_index("seq")
    c = lax.axis_index("ctx")
    rows = tok_own.shape[0]
    cols = w_v.shape[1]
    tiles = cols // col_tile
    docs = len_ref.shape[1]
    direct = cols % 128 == 0
    per_chunk = rows // chunks

    def up_of(k):
        return jnp.where(c + k < devices, c + k, 2 * devices - 1 - c - k)

    w_copies = [
        pltpu.make_async_copy(
            w_ref.at[:, pl.ds(t * col_tile, col_tile)],
            w_v.at[:, pl.ds(t * col_tile, col_tile)],
            local_sem.at[1 + t],
        )
        for t in range(tiles)
    ]
    own_copy = pltpu.make_async_copy(tok_ref.at[0], tok_own, local_sem.at[0])

    barrier = pltpu.get_barrier_semaphore()
    for j in range(1, parts):
        pl.semaphore_signal(
            barrier, inc=1, device_id=(lax.rem(me + j, parts), c), device_id_type=MESH
        )
    expected = jnp.int32(parts - 1)
    for k in range(1, steps + 1):
        up = up_of(k)
        expected = expected + (up != c).astype(jnp.int32) + (c >= k).astype(jnp.int32)

        @pl.when(up != c)
        def _():
            pl.semaphore_signal(barrier, inc=1, device_id=(me, up), device_id_type=MESH)

        @pl.when(c >= k)
        def _():
            pl.semaphore_signal(barrier, inc=1, device_id=(me, c - k), device_id_type=MESH)

    own_copy.start()
    for t in reversed(range(tiles)):
        w_copies[t].start()
    pl.semaphore_wait(barrier, expected)

    def token_copy(j, h):
        part = pl.ds(h * per_chunk, per_chunk)
        return pltpu.make_async_remote_copy(
            src_ref=tok_ref.at[0, part],
            dst_ref=tok_in.at[j - 1, part],
            send_sem=tok_send.at[j - 1, h],
            recv_sem=tok_recv.at[j - 1, h],
            device_id=(lax.rem(me + j, parts), c),
            device_id_type=MESH,
        )

    def back_copy(j, h, t):
        part = pl.ds(h * per_chunk, per_chunk)
        lanes = pl.ds(t * col_tile, col_tile)
        if direct:
            start = pl.multiple_of(me * cols + t * col_tile, 128)
            target = full.at[part, pl.ds(start, col_tile)]
        else:
            target = pieces.at[me, part]
        return pltpu.make_async_remote_copy(
            src_ref=back.at[j - 1, part, lanes],
            dst_ref=target,
            send_sem=back_send.at[j - 1, h, t],
            recv_sem=back_recv.at[j - 1, h, t],
            device_id=(lax.rem(me + parts - j, parts), c),
            device_id_type=MESH,
        )

    for h in range(chunks):
        for j in range(1, parts):
            token_copy(j, h).start()

    row = lax.broadcasted_iota(jnp.int32, (SPAN, PAIR), 0)
    lane = lax.broadcasted_iota(jnp.int32, (SPAN, PAIR), 1)
    first_half = lax.rem(lane, HEAD_SIZE) < HEAD_SIZE // 2
    low = lane < HEAD_SIZE
    firsts = (c, 2 * devices - 1 - c)
    total_keys = (steps + 1) * SPAN
    for e in range(2):
        angle = (row + firsts[e] * SPAN).astype(jnp.float32) * freq_ref[...]
        cos_s[e] = jnp.cos(angle)
        sine = jnp.sin(angle)
        sin_s[e] = jnp.where(first_half, -sine, sine)
        key_at = lax.broadcasted_iota(jnp.int32, (SPAN, total_keys), 1)
        block = key_at // SPAN
        key_place = (firsts[e] - block) * SPAN + key_at - block * SPAN
        q_place = lax.broadcasted_iota(jnp.int32, (SPAN, total_keys), 0) + firsts[e] * SPAN
        doc_start = jnp.zeros((SPAN, total_keys), jnp.int32)
        end = jnp.int32(0)
        for d in range(docs):
            end = end + len_ref[0, d]
            doc_start = jnp.where(q_place >= end, end, doc_start)
        live = (key_place >= doc_start) & (key_place <= q_place)
        bias[e] = jnp.where(live, 0.0, -1e30)
    for k in range(1, steps + 1):

        @pl.when(c < k)
        def _():
            kv[0, k] = jnp.zeros((SPAN, 2 * KVCOLS), kv.dtype)

    def project(value, t):
        return jnp.dot(
            value, w_v[:, t * col_tile : (t + 1) * col_tile], preferred_element_type=jnp.float32
        ).astype(jnp.bfloat16)

    own_copy.wait()
    for t in reversed(range(tiles)):
        w_copies[t].wait()
        value = project(tok_own[...], t)
        if direct:
            start = pl.multiple_of(me * cols + t * col_tile, 128)
            full[:, pl.ds(start, col_tile)] = value
        else:
            pieces[me] = value

    for h in range(chunks):
        part = slice(h * per_chunk, (h + 1) * per_chunk)
        for j in range(1, parts):
            token_copy(j, h).wait_recv()
            for t in reversed(range(tiles)):
                back[j - 1, part, t * col_tile : (t + 1) * col_tile] = project(
                    tok_in[j - 1, part], t
                )
                back_copy(j, h, t).start()

    for t in reversed(range(tiles)):
        for h in range(chunks):
            for j in range(1, parts):
                back_copy(j, h, t).wait_recv()
    if not direct:
        for p in range(parts):
            full[:, p * cols : (p + 1) * cols] = pieces[p]

    flip = jnp.full((SPAN, PAIR), order_ref[0, 2 * c], jnp.int32) >= devices

    def pair_of(column):
        block = full[:, column : column + PAIR].astype(jnp.float32)
        one, two = block[:SPAN], block[SPAN:]
        return jnp.where(flip, two, one), jnp.where(flip, one, two)

    def turn(value, e):
        other = jnp.where(
            first_half, pltpu.roll(value, PAIR - HEAD_SIZE // 2, 1), pltpu.roll(value, HEAD_SIZE // 2, 1)
        )
        return value * cos_s[e] + other * sin_s[e]

    for b in range(KVCOLS // PAIR):
        both = pair_of(QCOLS + b * PAIR)
        values = pair_of(QCOLS + KVCOLS + b * PAIR)
        for e in range(2):
            kv[e, 0, :, b * PAIR : (b + 1) * PAIR] = turn(both[e], e).astype(jnp.bfloat16)
            kv[e, 0, :, KVCOLS + b * PAIR : KVCOLS + (b + 1) * PAIR] = values[e].astype(jnp.bfloat16)

    def early_copy(k):
        wrapped = (c + k >= devices).astype(jnp.int32)
        return pltpu.make_async_remote_copy(
            src_ref=kv.at[0, 0],
            dst_ref=kv.at[wrapped, k],
            send_sem=kv_send.at[0, k - 1],
            recv_sem=kv_recv.at[wrapped, k - 1],
            device_id=(me, up_of(k)),
            device_id_type=MESH,
        )

    def late_copy(k):
        return pltpu.make_async_remote_copy(
            src_ref=kv.at[1, 0],
            dst_ref=kv.at[1, k],
            send_sem=kv_send.at[1, k - 1],
            recv_sem=kv_recv.at[1, k - 1],
            device_id=(me, jnp.maximum(c - k, 0)),
            device_id_type=MESH,
        )

    def arrival(e, k):
        return pltpu.make_async_remote_copy(
            src_ref=kv.at[e, 0],
            dst_ref=kv.at[e, k],
            send_sem=kv_send.at[e, k - 1],
            recv_sem=kv_recv.at[e, k - 1],
            device_id=(me, up_of(k)),
            device_id_type=MESH,
        )

    for k in reversed(range(1, steps + 1)):

        @pl.when(up_of(k) != c)
        def _():
            early_copy(k).start()

        @pl.when(c >= k)
        def _():
            late_copy(k).start()

        @pl.when(up_of(k) == c)
        def _():
            kv[1, k] = kv[0, 0]

    for b in range(QCOLS // PAIR):
        both = pair_of(b * PAIR)
        g = 2 * b // QUERY_PER_KV
        for e in range(2):
            turned = turn(both[e], e)
            swapped = pltpu.roll(turned, HEAD_SIZE, 1)
            for s in range(2):
                i = (2 * b + s) % QUERY_PER_KV
                placed = turned if s == g % 2 else swapped
                keep = low if g % 2 == 0 else ~low
                q_s[e, g, i * SPAN : (i + 1) * SPAN] = jnp.where(keep, placed, 0.0).astype(
                    jnp.bfloat16
                )

    for k in range(1, steps + 1):

        @pl.when(c >= k)
        def _():
            arrival(0, k).wait_recv()

        @pl.when(up_of(k) != c)
        def _():
            arrival(1, k).wait_recv()

    for g in range(KEY_VALUE_HEADS):
        pair = (g // 2) * PAIR
        outs = []
        for e in range(2):
            keys = kv[e, :, :, pair : pair + PAIR].reshape(total_keys, PAIR)
            values = kv[e, :, :, KVCOLS + pair : KVCOLS + pair + PAIR].reshape(total_keys, PAIR)
            scores = lax.dot_general(
                q_s[e, g], keys, (((1,), (1,)), ((), ())), preferred_element_type=jnp.float32
            )
            scores = scores.reshape(QUERY_PER_KV, SPAN, total_keys) * SCALE + bias[e][None]
            scores = scores.reshape(QUERY_PER_KV * SPAN, total_keys)
            top = jnp.max(scores, axis=1, keepdims=True)
            weights = jnp.exp2(scores - top)
            total = jnp.sum(weights, axis=1, keepdims=True)
            summed = jnp.dot(
                weights.astype(jnp.bfloat16), values, preferred_element_type=jnp.float32
            )
            outs.append(summed / total)
        for m in range(QUERY_PER_KV // 2):
            made = []
            for e in range(2):
                one = outs[e][(2 * m) * SPAN : (2 * m + 1) * SPAN]
                two = outs[e][(2 * m + 1) * SPAN : (2 * m + 2) * SPAN]
                if g % 2 == 0:
                    two = pltpu.roll(two, HEAD_SIZE, 1)
                else:
                    one = pltpu.roll(one, HEAD_SIZE, 1)
                made.append(jnp.where(low, one, two))
            at = (g * QUERY_PER_KV + 2 * m) * HEAD_SIZE
            out_ref[0, :SPAN, at : at + PAIR] = jnp.where(flip, made[1], made[0]).astype(jnp.bfloat16)
            out_ref[0, SPAN:, at : at + PAIR] = jnp.where(flip, made[0], made[1]).astype(jnp.bfloat16)

    for j in range(1, parts):
        for h in range(chunks):
            token_copy(j, h).wait_send()
            for t in range(tiles):
                back_copy(j, h, t).wait_send()
    for k in range(1, steps + 1):

        @pl.when(up_of(k) != c)
        def _():
            early_copy(k).wait_send()

        @pl.when(c >= k)
        def _():
            late_copy(k).wait_send()


def body(parts, devices, tokens, qkv_weight, doc_lengths, span_order):
    _, rows, width = tokens.shape
    cols = qkv_weight.shape[1]
    steps = devices // 4
    chunks = 2
    col_tile = 256 if cols % 256 == 0 else cols
    tiles = cols // col_tile
    half = HEAD_SIZE // 2
    freq = 500000.0 ** (-np.arange(half, dtype=np.float64) * 2.0 / HEAD_SIZE)
    freq = np.tile(freq.astype(np.float32), PAIR // half)[None]
    pieces_shape = (parts, rows, cols) if cols % 128 else (1, 16, 128)
    return pl.pallas_call(
        functools.partial(kernel, parts, devices, steps, chunks, col_tile),
        out_shape=jax.ShapeDtypeStruct((1, rows, QCOLS), jnp.bfloat16),
        in_specs=[
            pl.BlockSpec(memory_space=pl.ANY),
            pl.BlockSpec(memory_space=pl.ANY),
            pl.BlockSpec(memory_space=pltpu.VMEM),
            pl.BlockSpec(memory_space=pltpu.SMEM),
            pl.BlockSpec(memory_space=pltpu.SMEM),
        ],
        out_specs=pl.BlockSpec(memory_space=pltpu.VMEM),
        scratch_shapes=[
            pltpu.VMEM((rows, width), jnp.bfloat16),
            pltpu.VMEM((width, cols), jnp.bfloat16),
            pltpu.VMEM((parts - 1, rows, width), jnp.bfloat16),
            pltpu.VMEM((parts - 1, rows, cols), jnp.bfloat16),
            pltpu.VMEM((rows, parts * cols), jnp.bfloat16),
            pltpu.VMEM(pieces_shape, jnp.bfloat16),
            pltpu.VMEM((2, steps + 1, SPAN, 2 * KVCOLS), jnp.bfloat16),
            pltpu.VMEM((2, KEY_VALUE_HEADS, QUERY_PER_KV * SPAN, PAIR), jnp.bfloat16),
            pltpu.VMEM((2, SPAN, (steps + 1) * SPAN), jnp.float32),
            pltpu.VMEM((2, SPAN, PAIR), jnp.float32),
            pltpu.VMEM((2, SPAN, PAIR), jnp.float32),
            pltpu.SemaphoreType.DMA((1 + tiles,)),
            pltpu.SemaphoreType.DMA((parts - 1, chunks)),
            pltpu.SemaphoreType.DMA((parts - 1, chunks)),
            pltpu.SemaphoreType.DMA((parts - 1, chunks, tiles)),
            pltpu.SemaphoreType.DMA((parts - 1, chunks, tiles)),
            pltpu.SemaphoreType.DMA((2, steps)),
            pltpu.SemaphoreType.DMA((2, steps)),
        ],
        compiler_params=pltpu.CompilerParams(
            collective_id=0, has_side_effects=True, vmem_limit_bytes=48 * 1024 * 1024
        ),
    )(tokens, qkv_weight, jnp.asarray(freq), doc_lengths, span_order)


def solution(mesh):
    placed = (P("seq", "ctx", None), P(None, "seq"), P("seq", None), P("seq", None))
    return jax.shard_map(
        functools.partial(body, mesh.shape["seq"], mesh.shape["ctx"]),
        mesh=mesh,
        in_specs=placed,
        out_specs=P("seq", "ctx", None),
        check_vma=False,
    )
```

```python
import functools
import math

import jax
import jax.numpy as jnp
import numpy as np
from jax import lax
from jax.experimental import pallas as pl
from jax.experimental.pallas import tpu as pltpu
from jax.sharding import PartitionSpec as P

QUERY_HEADS = 16
KEY_VALUE_HEADS = 4
HEAD_SIZE = 64
QUERY_PER_KV = 4
SPAN = 64
PAIR = 2 * HEAD_SIZE
QCOLS = QUERY_HEADS * HEAD_SIZE
KVCOLS = KEY_VALUE_HEADS * HEAD_SIZE
MESH = pl.DeviceIdType.MESH
SCALE = 0.125 * math.log2(math.e)


def kernel(
    parts, devices, steps, chunks, ahead, col_tile,
    tok_ref, w_ref, freq_ref, len_ref, order_ref, out_ref,
    tok_raw, tok_own, w_v, tok_in, back, full, pieces, kv, q_s, bias, cos_s, sin_s, out_s,
    local_sem, tok_send, tok_recv, back_send, back_recv, kv_send, kv_recv,
):
    me = lax.axis_index("seq")
    c = lax.axis_index("ctx")
    rows = tok_own.shape[0]
    cols = w_v.shape[1]
    tiles = cols // col_tile
    docs = len_ref.shape[1]
    direct = cols % 128 == 0
    per_chunk = rows // chunks
    per_span = chunks // 2

    def up_of(k):
        return jnp.where(c + k < devices, c + k, 2 * devices - 1 - c - k)

    order_mine = order_ref[0, 2 * c]

    def choose(one, two):
        swap = jnp.full(one.shape, order_mine, jnp.int32) >= devices
        one, two = one.astype(jnp.float32), two.astype(jnp.float32)
        return jnp.where(swap, two, one).astype(jnp.bfloat16)

    w_copies = [
        pltpu.make_async_copy(
            w_ref.at[:, pl.ds(t * col_tile, col_tile)],
            w_v.at[:, pl.ds(t * col_tile, col_tile)],
            local_sem.at[1 + t],
        )
        for t in range(tiles)
    ]
    raw_copy = pltpu.make_async_copy(tok_ref.at[0], tok_raw, local_sem.at[0])
    raw_copy.start()

    barrier = pltpu.get_barrier_semaphore()
    for j in range(1, parts):
        pl.semaphore_signal(
            barrier, inc=1, device_id=(lax.rem(me + j, parts), c), device_id_type=MESH
        )
    expected = jnp.int32(parts - 1)
    for k in range(1, steps + 1):
        up = up_of(k)
        expected = expected + (up != c).astype(jnp.int32) + (c >= k).astype(jnp.int32)

        @pl.when(up != c)
        def _():
            pl.semaphore_signal(barrier, inc=1, device_id=(me, up), device_id_type=MESH)

        @pl.when(c >= k)
        def _():
            pl.semaphore_signal(barrier, inc=1, device_id=(me, c - k), device_id_type=MESH)

    raw_copy.wait()
    for t in reversed(range(tiles)):
        w_copies[t].start()
    tok_own[:SPAN] = choose(tok_raw[:SPAN], tok_raw[SPAN:])
    tok_own[SPAN:] = choose(tok_raw[SPAN:], tok_raw[:SPAN])
    pl.semaphore_wait(barrier, expected)

    def token_copy(j, h):
        part = pl.ds(h * per_chunk, per_chunk)
        return pltpu.make_async_remote_copy(
            src_ref=tok_own.at[part],
            dst_ref=tok_in.at[j - 1, part],
            send_sem=tok_send.at[j - 1, h],
            recv_sem=tok_recv.at[j - 1, h],
            device_id=(lax.rem(me + j, parts), c),
            device_id_type=MESH,
        )

    def back_copy(j, h, t):
        part = pl.ds(h * per_chunk, per_chunk)
        lanes = pl.ds(t * col_tile, col_tile)
        if direct:
            start = pl.multiple_of(me * cols + t * col_tile, 128)
            target = full.at[part, pl.ds(start, col_tile)]
        else:
            target = pieces.at[me, part]
        return pltpu.make_async_remote_copy(
            src_ref=back.at[j - 1, part, lanes],
            dst_ref=target,
            send_sem=back_send.at[j - 1, h, t],
            recv_sem=back_recv.at[j - 1, h, t],
            device_id=(lax.rem(me + parts - j, parts), c),
            device_id_type=MESH,
        )

    def send_tokens(h):
        for j in range(1, parts):
            token_copy(j, h).start()

    for h in range(min(ahead, chunks)):
        send_tokens(h)

    row = lax.broadcasted_iota(jnp.int32, (SPAN, PAIR), 0)
    firsts = (c, 2 * devices - 1 - c)
    total_keys = (steps + 1) * SPAN

    def half_masks(count):
        lane = lax.broadcasted_iota(jnp.int32, (count, PAIR), 1)
        return lax.rem(lane, HEAD_SIZE) < HEAD_SIZE // 2, lane < HEAD_SIZE

    first_half, low = half_masks(SPAN)
    for e in range(2):
        angle = (row + firsts[e] * SPAN).astype(jnp.float32) * freq_ref[...]
        cos_s[e] = jnp.cos(angle)
        sine = jnp.sin(angle)
        sin_s[e] = jnp.where(first_half, -sine, sine)
        key_at = lax.broadcasted_iota(jnp.int32, (SPAN, total_keys), 1)
        block = key_at // SPAN
        key_place = (firsts[e] - block) * SPAN + key_at - block * SPAN
        q_place = lax.broadcasted_iota(jnp.int32, (SPAN, total_keys), 0) + firsts[e] * SPAN
        doc_start = jnp.zeros((SPAN, total_keys), jnp.int32)
        end = jnp.int32(0)
        for d in range(docs):
            end = end + len_ref[0, d]
            doc_start = jnp.where(q_place >= end, end, doc_start)
        live = (key_place >= doc_start) & (key_place <= q_place)
        bias[e] = jnp.where(live, 0.0, -1e30)
    for k in range(1, steps + 1):

        @pl.when(c < k)
        def _():
            kv[0, k] = jnp.zeros((SPAN, 2 * KVCOLS), kv.dtype)

    def project(value, t):
        return jnp.dot(
            value, w_v[:, t * col_tile : (t + 1) * col_tile], preferred_element_type=jnp.float32
        ).astype(jnp.bfloat16)

    for t in reversed(range(tiles)):
        w_copies[t].wait()
        value = project(tok_own[...], t)
        if direct:
            start = pl.multiple_of(me * cols + t * col_tile, 128)
            full[:, pl.ds(start, col_tile)] = value
        else:
            pieces[me] = value

    def serve(h):
        part = slice(h * per_chunk, (h + 1) * per_chunk)
        for j in range(1, parts):
            token_copy(j, h).wait_recv()
            for t in reversed(range(tiles)):
                back[j - 1, part, t * col_tile : (t + 1) * col_tile] = project(
                    tok_in[j - 1, part], t
                )
                back_copy(j, h, t).start()

    def arrived_back(h, which):
        for t in which:
            for j in range(1, parts):
                back_copy(j, h, t).wait_recv()

    kv_tiles = [
        t
        for t in range(tiles)
        if any(p * cols + (t + 1) * col_tile > QCOLS for p in range(parts))
    ]
    q_tiles = [t for t in range(tiles) if t not in kv_tiles]

    def turn(value, e, at):
        count = value.shape[0]
        other = jnp.where(
            half_masks(count)[0],
            pltpu.roll(value, PAIR - HEAD_SIZE // 2, 1),
            pltpu.roll(value, HEAD_SIZE // 2, 1),
        )
        return value * cos_s[e, at : at + count] + other * sin_s[e, at : at + count]

    def early_copy(k, i):
        wrapped = (c + k >= devices).astype(jnp.int32)
        part = pl.ds(i * per_chunk, per_chunk)
        return pltpu.make_async_remote_copy(
            src_ref=kv.at[0, 0, part],
            dst_ref=kv.at[wrapped, k, part],
            send_sem=kv_send.at[0, k - 1, i],
            recv_sem=kv_recv.at[wrapped, k - 1, i],
            device_id=(me, up_of(k)),
            device_id_type=MESH,
        )

    def late_copy(k, i):
        part = pl.ds(i * per_chunk, per_chunk)
        return pltpu.make_async_remote_copy(
            src_ref=kv.at[1, 0, part],
            dst_ref=kv.at[1, k, part],
            send_sem=kv_send.at[1, k - 1, i],
            recv_sem=kv_recv.at[1, k - 1, i],
            device_id=(me, jnp.maximum(c - k, 0)),
            device_id_type=MESH,
        )

    def arrival(e, k, i):
        part = pl.ds(i * per_chunk, per_chunk)
        return pltpu.make_async_remote_copy(
            src_ref=kv.at[e, 0, part],
            dst_ref=kv.at[e, k, part],
            send_sem=kv_send.at[e, k - 1, i],
            recv_sem=kv_recv.at[e, k - 1, i],
            device_id=(me, up_of(k)),
            device_id_type=MESH,
        )

    def spread(h):
        e, i = h // per_span, h % per_span
        at = i * per_chunk
        part = slice(h * per_chunk, (h + 1) * per_chunk)
        arrived_back(h, kv_tiles)
        if not direct:
            for p in range(parts):
                full[part, p * cols : (p + 1) * cols] = pieces[p, part]
        for b in range(KVCOLS // PAIR):
            block = full[part, QCOLS + b * PAIR : QCOLS + (b + 1) * PAIR].astype(jnp.float32)
            kv[e, 0, at : at + per_chunk, b * PAIR : (b + 1) * PAIR] = turn(block, e, at).astype(
                jnp.bfloat16
            )
        kv[e, 0, at : at + per_chunk, KVCOLS:] = full[part, QCOLS + KVCOLS :]
        for k in reversed(range(1, steps + 1)):
            if e == 0:

                @pl.when(up_of(k) != c)
                def _():
                    early_copy(k, i).start()

            else:

                @pl.when(c >= k)
                def _():
                    late_copy(k, i).start()

    def queries(e):
        for i in range(per_span):
            arrived_back(e * per_span + i, q_tiles)
        for b in range(QCOLS // PAIR):
            block = full[e * SPAN : (e + 1) * SPAN, b * PAIR : (b + 1) * PAIR]
            turned = turn(block.astype(jnp.float32), e, 0)
            swapped = pltpu.roll(turned, HEAD_SIZE, 1)
            g = 2 * b // QUERY_PER_KV
            for s in range(2):
                i = (2 * b + s) % QUERY_PER_KV
                placed = turned if s == g % 2 else swapped
                keep = low if g % 2 == 0 else ~low
                q_s[e, g, i * SPAN : (i + 1) * SPAN] = jnp.where(keep, placed, 0.0).astype(
                    jnp.bfloat16
                )

    def attend(e):
        for g in range(KEY_VALUE_HEADS):
            pair = (g // 2) * PAIR
            keys = kv[e, :, :, pair : pair + PAIR].reshape(total_keys, PAIR)
            values = kv[e, :, :, KVCOLS + pair : KVCOLS + pair + PAIR].reshape(total_keys, PAIR)
            scores = lax.dot_general(
                q_s[e, g], keys, (((1,), (1,)), ((), ())), preferred_element_type=jnp.float32
            )
            scores = scores.reshape(QUERY_PER_KV, SPAN, total_keys) * SCALE + bias[e][None]
            scores = scores.reshape(QUERY_PER_KV * SPAN, total_keys)
            top = jnp.max(scores, axis=1, keepdims=True)
            weights = jnp.exp2(scores - top)
            total = jnp.sum(weights, axis=1, keepdims=True)
            summed = jnp.dot(
                weights.astype(jnp.bfloat16), values, preferred_element_type=jnp.float32
            )
            outs = summed / total
            for m in range(QUERY_PER_KV // 2):
                one = outs[(2 * m) * SPAN : (2 * m + 1) * SPAN]
                two = outs[(2 * m + 1) * SPAN : (2 * m + 2) * SPAN]
                if g % 2 == 0:
                    two = pltpu.roll(two, HEAD_SIZE, 1)
                else:
                    one = pltpu.roll(one, HEAD_SIZE, 1)
                at = (g * QUERY_PER_KV + 2 * m) * HEAD_SIZE
                out_s[e * SPAN : (e + 1) * SPAN, at : at + PAIR] = jnp.where(low, one, two).astype(
                    jnp.bfloat16
                )

    for h in range(chunks):
        serve(h)
        if h + ahead < chunks:
            send_tokens(h + ahead)
        if h >= 1:
            spread(h - 1)
        if h == chunks - 1:
            queries(0)
    spread(chunks - 1)

    for k in range(1, steps + 1):

        @pl.when(up_of(k) == c)
        def _():
            kv[1, k] = kv[0, 0]

    for k in range(1, steps + 1):

        @pl.when(c >= k)
        def _():
            for i in range(per_span):
                arrival(0, k, i).wait_recv()

    attend(0)
    queries(1)
    for k in range(1, steps + 1):

        @pl.when(up_of(k) != c)
        def _():
            for i in range(per_span):
                arrival(1, k, i).wait_recv()

    attend(1)
    out_ref[0, :SPAN] = choose(out_s[:SPAN], out_s[SPAN:])
    out_ref[0, SPAN:] = choose(out_s[SPAN:], out_s[:SPAN])

    for j in range(1, parts):
        for h in range(chunks):
            token_copy(j, h).wait_send()
            for t in range(tiles):
                back_copy(j, h, t).wait_send()
    for k in range(1, steps + 1):

        @pl.when(up_of(k) != c)
        def _():
            for i in range(per_span):
                early_copy(k, i).wait_send()

        @pl.when(c >= k)
        def _():
            for i in range(per_span):
                late_copy(k, i).wait_send()


def body(parts, devices, tokens, qkv_weight, doc_lengths, span_order):
    _, rows, width = tokens.shape
    cols = qkv_weight.shape[1]
    steps = devices // 4
    chunks = 4
    ahead = 3
    col_tile = 256 if cols % 256 == 0 else cols
    tiles = cols // col_tile
    half = HEAD_SIZE // 2
    freq = 500000.0 ** (-np.arange(half, dtype=np.float64) * 2.0 / HEAD_SIZE)
    freq = np.tile(freq.astype(np.float32), PAIR // half)[None]
    pieces_shape = (parts, rows, cols) if cols % 128 else (1, 16, 128)
    return pl.pallas_call(
        functools.partial(kernel, parts, devices, steps, chunks, ahead, col_tile),
        out_shape=jax.ShapeDtypeStruct((1, rows, QCOLS), jnp.bfloat16),
        in_specs=[
            pl.BlockSpec(memory_space=pl.ANY),
            pl.BlockSpec(memory_space=pl.ANY),
            pl.BlockSpec(memory_space=pltpu.VMEM),
            pl.BlockSpec(memory_space=pltpu.SMEM),
            pl.BlockSpec(memory_space=pltpu.SMEM),
        ],
        out_specs=pl.BlockSpec(memory_space=pltpu.VMEM),
        scratch_shapes=[
            pltpu.VMEM((rows, width), jnp.bfloat16),
            pltpu.VMEM((rows, width), jnp.bfloat16),
            pltpu.VMEM((width, cols), jnp.bfloat16),
            pltpu.VMEM((parts - 1, rows, width), jnp.bfloat16),
            pltpu.VMEM((parts - 1, rows, cols), jnp.bfloat16),
            pltpu.VMEM((rows, parts * cols), jnp.bfloat16),
            pltpu.VMEM(pieces_shape, jnp.bfloat16),
            pltpu.VMEM((2, steps + 1, SPAN, 2 * KVCOLS), jnp.bfloat16),
            pltpu.VMEM((2, KEY_VALUE_HEADS, QUERY_PER_KV * SPAN, PAIR), jnp.bfloat16),
            pltpu.VMEM((2, SPAN, (steps + 1) * SPAN), jnp.float32),
            pltpu.VMEM((2, SPAN, PAIR), jnp.float32),
            pltpu.VMEM((2, SPAN, PAIR), jnp.float32),
            pltpu.VMEM((rows, QCOLS), jnp.bfloat16),
            pltpu.SemaphoreType.DMA((1 + tiles,)),
            pltpu.SemaphoreType.DMA((parts - 1, chunks)),
            pltpu.SemaphoreType.DMA((parts - 1, chunks)),
            pltpu.SemaphoreType.DMA((parts - 1, chunks, tiles)),
            pltpu.SemaphoreType.DMA((parts - 1, chunks, tiles)),
            pltpu.SemaphoreType.DMA((2, steps, chunks // 2)),
            pltpu.SemaphoreType.DMA((2, steps, chunks // 2)),
        ],
        compiler_params=pltpu.CompilerParams(
            collective_id=0, has_side_effects=True, vmem_limit_bytes=62 * 1024 * 1024
        ),
    )(tokens, qkv_weight, jnp.asarray(freq), doc_lengths, span_order)


def solution(mesh):
    placed = (P("seq", "ctx", None), P(None, "seq"), P("seq", None), P("seq", None))
    return jax.shard_map(
        functools.partial(body, mesh.shape["seq"], mesh.shape["ctx"]),
        mesh=mesh,
        in_specs=placed,
        out_specs=P("seq", "ctx", None),
        check_vma=False,
    )
```

```python
import functools
import math

import jax
import jax.numpy as jnp
import numpy as np
from jax import lax
from jax.experimental import pallas as pl
from jax.experimental.pallas import tpu as pltpu
from jax.sharding import PartitionSpec as P

QUERY_HEADS = 16
KEY_VALUE_HEADS = 4
HEAD_SIZE = 64
QUERY_PER_KV = 4
SPAN = 64
PAIR = 2 * HEAD_SIZE
QCOLS = QUERY_HEADS * HEAD_SIZE
KVCOLS = KEY_VALUE_HEADS * HEAD_SIZE
MESH = pl.DeviceIdType.MESH
SCALE = 0.125 * math.log2(math.e)


def kernel(
    parts, devices, steps, chunks, ahead, col_tile,
    tok_ref, w_ref, len_ref, order_ref, out_ref,
    tok_raw, tok_own, w_v, tok_in, back, full, pieces, kv, q_s, bias, cos_s, sin_s, out_s,
    local_sem, tok_send, tok_recv, back_send, back_recv, kv_send, kv_recv,
):
    me = lax.axis_index("seq")
    c = lax.axis_index("ctx")
    rows = tok_own.shape[0]
    cols = w_v.shape[1]
    tiles = cols // col_tile
    docs = len_ref.shape[1]
    direct = cols % 128 == 0
    per_chunk = rows // chunks
    per_span = chunks // 2

    def up_of(k):
        return jnp.where(c + k < devices, c + k, 2 * devices - 1 - c - k)

    order_mine = order_ref[0, 2 * c]

    def choose(one, two):
        swap = jnp.full(one.shape, order_mine, jnp.int32) >= devices
        one, two = one.astype(jnp.float32), two.astype(jnp.float32)
        return jnp.where(swap, two, one).astype(jnp.bfloat16)

    w_copies = [
        pltpu.make_async_copy(
            w_ref.at[:, pl.ds(t * col_tile, col_tile)],
            w_v.at[:, pl.ds(t * col_tile, col_tile)],
            local_sem.at[1 + t],
        )
        for t in range(tiles)
    ]
    raw_copy = pltpu.make_async_copy(tok_ref.at[0], tok_raw, local_sem.at[0])
    raw_copy.start()

    barrier = pltpu.get_barrier_semaphore()
    for j in range(1, parts):
        pl.semaphore_signal(
            barrier, inc=1, device_id=(lax.rem(me + j, parts), c), device_id_type=MESH
        )
    expected = jnp.int32(parts - 1)
    for k in range(1, steps + 1):
        up = up_of(k)
        expected = expected + (up != c).astype(jnp.int32) + (c >= k).astype(jnp.int32)

        @pl.when(up != c)
        def _():
            pl.semaphore_signal(barrier, inc=1, device_id=(me, up), device_id_type=MESH)

        @pl.when(c >= k)
        def _():
            pl.semaphore_signal(barrier, inc=1, device_id=(me, c - k), device_id_type=MESH)

    raw_copy.wait()
    for t in reversed(range(tiles)):
        w_copies[t].start()
    tok_own[:SPAN] = choose(tok_raw[:SPAN], tok_raw[SPAN:])
    tok_own[SPAN:] = choose(tok_raw[SPAN:], tok_raw[:SPAN])
    pl.semaphore_wait(barrier, expected)

    def token_copy(j, h):
        part = pl.ds(h * per_chunk, per_chunk)
        return pltpu.make_async_remote_copy(
            src_ref=tok_own.at[part],
            dst_ref=tok_in.at[j - 1, part],
            send_sem=tok_send.at[j - 1, h],
            recv_sem=tok_recv.at[j - 1, h],
            device_id=(lax.rem(me + j, parts), c),
            device_id_type=MESH,
        )

    def back_copy(j, h, t):
        part = pl.ds(h * per_chunk, per_chunk)
        lanes = pl.ds(t * col_tile, col_tile)
        if direct:
            start = pl.multiple_of(me * cols + t * col_tile, 128)
            target = full.at[part, pl.ds(start, col_tile)]
        else:
            target = pieces.at[me, part]
        return pltpu.make_async_remote_copy(
            src_ref=back.at[j - 1, part, lanes],
            dst_ref=target,
            send_sem=back_send.at[j - 1, h, t],
            recv_sem=back_recv.at[j - 1, h, t],
            device_id=(lax.rem(me + parts - j, parts), c),
            device_id_type=MESH,
        )

    def send_tokens(h):
        for j in range(1, parts):
            token_copy(j, h).start()

    split = direct and (parts - 1) * cols <= QCOLS
    last = me == parts - 1
    for h in range(min(ahead, chunks)):
        send_tokens(h)
    if split:

        @pl.when(jnp.logical_not(last))
        def _():
            for h in range(ahead, chunks):
                send_tokens(h)

    row = lax.broadcasted_iota(jnp.int32, (SPAN, PAIR), 0)
    firsts = (c, 2 * devices - 1 - c)
    total_keys = (steps + 1) * SPAN

    def half_masks(count):
        lane = lax.broadcasted_iota(jnp.int32, (count, PAIR), 1)
        return lax.rem(lane, HEAD_SIZE) < HEAD_SIZE // 2, lane < HEAD_SIZE

    first_half, low = half_masks(SPAN)
    index = lax.rem(lax.broadcasted_iota(jnp.int32, (1, PAIR), 1), HEAD_SIZE // 2)
    freq = jnp.zeros((1, PAIR), jnp.float32)
    for i in range(HEAD_SIZE // 2):
        freq = jnp.where(index == i, np.float32(500000.0 ** (-2.0 * i / HEAD_SIZE)), freq)
    for e in range(2):
        angle = (row + firsts[e] * SPAN).astype(jnp.float32) * freq
        cos_s[e] = jnp.cos(angle)
        sine = jnp.sin(angle)
        sin_s[e] = jnp.where(first_half, -sine, sine)
        key_at = lax.broadcasted_iota(jnp.int32, (SPAN, total_keys), 1)
        block = key_at // SPAN
        key_place = (firsts[e] - block) * SPAN + key_at - block * SPAN
        q_place = lax.broadcasted_iota(jnp.int32, (SPAN, total_keys), 0) + firsts[e] * SPAN
        doc_start = jnp.zeros((SPAN, total_keys), jnp.int32)
        end = jnp.int32(0)
        for d in range(docs):
            end = end + len_ref[0, d]
            doc_start = jnp.where(q_place >= end, end, doc_start)
        live = (key_place >= doc_start) & (key_place <= q_place)
        bias[e] = jnp.where(live, 0.0, -1e30)
    for k in range(1, steps + 1):

        @pl.when(c < k)
        def _():
            kv[0, k] = jnp.zeros((SPAN, 2 * KVCOLS), kv.dtype)

    def project(value, t):
        return jnp.dot(
            value, w_v[:, t * col_tile : (t + 1) * col_tile], preferred_element_type=jnp.float32
        ).astype(jnp.bfloat16)

    for t in reversed(range(tiles)):
        w_copies[t].wait()
        value = project(tok_own[...], t)
        if direct:
            start = pl.multiple_of(me * cols + t * col_tile, 128)
            full[:, pl.ds(start, col_tile)] = value
        else:
            pieces[me] = value

    def serve(h):
        part = slice(h * per_chunk, (h + 1) * per_chunk)
        for j in range(1, parts):
            token_copy(j, h).wait_recv()
            for t in reversed(range(tiles)):
                back[j - 1, part, t * col_tile : (t + 1) * col_tile] = project(
                    tok_in[j - 1, part], t
                )
                back_copy(j, h, t).start()

    def arrived_back(h, which):
        for t in which:
            for j in range(1, parts):
                back_copy(j, h, t).wait_recv()

    kv_tiles = [
        t
        for t in range(tiles)
        if any(p * cols + (t + 1) * col_tile > QCOLS for p in range(parts))
    ]
    q_tiles = [t for t in range(tiles) if t not in kv_tiles]

    def turn(value, e, at):
        count = value.shape[0]
        other = jnp.where(
            half_masks(count)[0],
            pltpu.roll(value, PAIR - HEAD_SIZE // 2, 1),
            pltpu.roll(value, HEAD_SIZE // 2, 1),
        )
        return value * cos_s[e, at : at + count] + other * sin_s[e, at : at + count]

    def early_copy(k, i):
        wrapped = (c + k >= devices).astype(jnp.int32)
        part = pl.ds(i * per_chunk, per_chunk)
        return pltpu.make_async_remote_copy(
            src_ref=kv.at[0, 0, part],
            dst_ref=kv.at[wrapped, k, part],
            send_sem=kv_send.at[0, k - 1, i],
            recv_sem=kv_recv.at[wrapped, k - 1, i],
            device_id=(me, up_of(k)),
            device_id_type=MESH,
        )

    def late_copy(k, i):
        part = pl.ds(i * per_chunk, per_chunk)
        return pltpu.make_async_remote_copy(
            src_ref=kv.at[1, 0, part],
            dst_ref=kv.at[1, k, part],
            send_sem=kv_send.at[1, k - 1, i],
            recv_sem=kv_recv.at[1, k - 1, i],
            device_id=(me, jnp.maximum(c - k, 0)),
            device_id_type=MESH,
        )

    def arrival(e, k, i):
        part = pl.ds(i * per_chunk, per_chunk)
        return pltpu.make_async_remote_copy(
            src_ref=kv.at[e, 0, part],
            dst_ref=kv.at[e, k, part],
            send_sem=kv_send.at[e, k - 1, i],
            recv_sem=kv_recv.at[e, k - 1, i],
            device_id=(me, up_of(k)),
            device_id_type=MESH,
        )

    def spread(h, which):
        e, i = h // per_span, h % per_span
        at = i * per_chunk
        part = slice(h * per_chunk, (h + 1) * per_chunk)
        arrived_back(h, which)
        if not direct:
            for p in range(parts):
                full[part, p * cols : (p + 1) * cols] = pieces[p, part]
        for b in range(KVCOLS // PAIR):
            block = full[part, QCOLS + b * PAIR : QCOLS + (b + 1) * PAIR].astype(jnp.float32)
            kv[e, 0, at : at + per_chunk, b * PAIR : (b + 1) * PAIR] = turn(block, e, at).astype(
                jnp.bfloat16
            )
        kv[e, 0, at : at + per_chunk, KVCOLS:] = full[part, QCOLS + KVCOLS :]
        for k in reversed(range(1, steps + 1)):
            if e == 0:

                @pl.when(up_of(k) != c)
                def _():
                    early_copy(k, i).start()

            else:

                @pl.when(c >= k)
                def _():
                    late_copy(k, i).start()

    def queries(e):
        def rest(which):
            for i in range(per_span):
                arrived_back(e * per_span + i, which)

        if split:
            pl.when(last)(lambda: rest(range(tiles)))
            pl.when(jnp.logical_not(last))(lambda: rest(q_tiles))
        else:
            rest(q_tiles)
        for b in range(QCOLS // PAIR):
            block = full[e * SPAN : (e + 1) * SPAN, b * PAIR : (b + 1) * PAIR]
            turned = turn(block.astype(jnp.float32), e, 0)
            swapped = pltpu.roll(turned, HEAD_SIZE, 1)
            g = 2 * b // QUERY_PER_KV
            for s in range(2):
                i = (2 * b + s) % QUERY_PER_KV
                placed = turned if s == g % 2 else swapped
                keep = low if g % 2 == 0 else ~low
                q_s[e, g, i * SPAN : (i + 1) * SPAN] = jnp.where(keep, placed, 0.0).astype(
                    jnp.bfloat16
                )

    def attend(e):
        for g in range(KEY_VALUE_HEADS):
            pair = (g // 2) * PAIR
            keys = kv[e, :, :, pair : pair + PAIR].reshape(total_keys, PAIR)
            values = kv[e, :, :, KVCOLS + pair : KVCOLS + pair + PAIR].reshape(total_keys, PAIR)
            scores = lax.dot_general(
                q_s[e, g], keys, (((1,), (1,)), ((), ())), preferred_element_type=jnp.float32
            )
            scores = scores.reshape(QUERY_PER_KV, SPAN, total_keys) * SCALE + bias[e][None]
            scores = scores.reshape(QUERY_PER_KV * SPAN, total_keys)
            top = jnp.max(scores, axis=1, keepdims=True)
            weights = jnp.exp2(scores - top)
            total = jnp.sum(weights, axis=1, keepdims=True)
            summed = jnp.dot(
                weights.astype(jnp.bfloat16), values, preferred_element_type=jnp.float32
            )
            outs = summed / total
            for m in range(QUERY_PER_KV // 2):
                one = outs[(2 * m) * SPAN : (2 * m + 1) * SPAN]
                two = outs[(2 * m + 1) * SPAN : (2 * m + 2) * SPAN]
                if g % 2 == 0:
                    two = pltpu.roll(two, HEAD_SIZE, 1)
                else:
                    one = pltpu.roll(one, HEAD_SIZE, 1)
                at = (g * QUERY_PER_KV + 2 * m) * HEAD_SIZE
                out_s[e * SPAN : (e + 1) * SPAN, at : at + PAIR] = jnp.where(low, one, two).astype(
                    jnp.bfloat16
                )

    if split:

        @pl.when(last)
        def _():
            for h in range(chunks):
                spread(h, [])
            for h in range(chunks):
                serve(h)
                if h + ahead < chunks:
                    send_tokens(h + ahead)

        @pl.when(jnp.logical_not(last))
        def _():
            for h in range(chunks):
                if h < chunks - 1:
                    serve(h)
                spread(h, kv_tiles)
            serve(chunks - 1)

        queries(0)
    else:
        for h in range(chunks):
            serve(h)
            if h + ahead < chunks:
                send_tokens(h + ahead)
            if h >= 1:
                spread(h - 1, kv_tiles)
        spread(chunks - 1, kv_tiles)
        queries(0)

    for k in range(1, steps + 1):

        @pl.when(up_of(k) == c)
        def _():
            kv[1, k] = kv[0, 0]

    for k in range(1, steps + 1):

        @pl.when(c >= k)
        def _():
            for i in range(per_span):
                arrival(0, k, i).wait_recv()

    attend(0)
    queries(1)
    for k in range(1, steps + 1):

        @pl.when(up_of(k) != c)
        def _():
            for i in range(per_span):
                arrival(1, k, i).wait_recv()

    attend(1)
    out_ref[0, :SPAN] = choose(out_s[:SPAN], out_s[SPAN:])
    out_ref[0, SPAN:] = choose(out_s[SPAN:], out_s[:SPAN])

    for j in range(1, parts):
        for h in range(chunks):
            token_copy(j, h).wait_send()
            for t in range(tiles):
                back_copy(j, h, t).wait_send()
    for k in range(1, steps + 1):

        @pl.when(up_of(k) != c)
        def _():
            for i in range(per_span):
                early_copy(k, i).wait_send()

        @pl.when(c >= k)
        def _():
            for i in range(per_span):
                late_copy(k, i).wait_send()


def body(parts, devices, tokens, qkv_weight, doc_lengths, span_order):
    _, rows, width = tokens.shape
    cols = qkv_weight.shape[1]
    steps = devices // 4
    chunks = 4
    ahead = 2
    col_tile = 256 if cols % 256 == 0 else cols
    tiles = cols // col_tile
    pieces_shape = (parts, rows, cols) if cols % 128 else (1, 16, 128)
    return pl.pallas_call(
        functools.partial(kernel, parts, devices, steps, chunks, ahead, col_tile),
        out_shape=jax.ShapeDtypeStruct((1, rows, QCOLS), jnp.bfloat16),
        in_specs=[
            pl.BlockSpec(memory_space=pl.ANY),
            pl.BlockSpec(memory_space=pl.ANY),
            pl.BlockSpec(memory_space=pltpu.SMEM),
            pl.BlockSpec(memory_space=pltpu.SMEM),
        ],
        out_specs=pl.BlockSpec(memory_space=pltpu.VMEM),
        scratch_shapes=[
            pltpu.VMEM((rows, width), jnp.bfloat16),
            pltpu.VMEM((rows, width), jnp.bfloat16),
            pltpu.VMEM((width, cols), jnp.bfloat16),
            pltpu.VMEM((parts - 1, rows, width), jnp.bfloat16),
            pltpu.VMEM((parts - 1, rows, cols), jnp.bfloat16),
            pltpu.VMEM((rows, parts * cols), jnp.bfloat16),
            pltpu.VMEM(pieces_shape, jnp.bfloat16),
            pltpu.VMEM((2, steps + 1, SPAN, 2 * KVCOLS), jnp.bfloat16),
            pltpu.VMEM((2, KEY_VALUE_HEADS, QUERY_PER_KV * SPAN, PAIR), jnp.bfloat16),
            pltpu.VMEM((2, SPAN, (steps + 1) * SPAN), jnp.float32),
            pltpu.VMEM((2, SPAN, PAIR), jnp.float32),
            pltpu.VMEM((2, SPAN, PAIR), jnp.float32),
            pltpu.VMEM((rows, QCOLS), jnp.bfloat16),
            pltpu.SemaphoreType.DMA((1 + tiles,)),
            pltpu.SemaphoreType.DMA((parts - 1, chunks)),
            pltpu.SemaphoreType.DMA((parts - 1, chunks)),
            pltpu.SemaphoreType.DMA((parts - 1, chunks, tiles)),
            pltpu.SemaphoreType.DMA((parts - 1, chunks, tiles)),
            pltpu.SemaphoreType.DMA((2, steps, chunks // 2)),
            pltpu.SemaphoreType.DMA((2, steps, chunks // 2)),
        ],
        compiler_params=pltpu.CompilerParams(
            collective_id=0, has_side_effects=True, vmem_limit_bytes=62 * 1024 * 1024
        ),
    )(tokens, qkv_weight, doc_lengths, span_order)


def solution(mesh):
    placed = (P("seq", "ctx", None), P(None, "seq"), P("seq", None), P("seq", None))
    return jax.shard_map(
        functools.partial(body, mesh.shape["seq"], mesh.shape["ctx"]),
        mesh=mesh,
        in_specs=placed,
        out_specs=P("seq", "ctx", None),
        check_vma=False,
    )
```
